32 devices in a mesh: dp: 8 (over z, x), expert: 4 (over y, core).
Axes of the slice: x: 2, y: 2, z: 4, core: 2. Of those that a mesh axis runs over, the one named last changes fastest.
Arguments:
- tokens_in: bfloat16 [2, 8192, 768], P(None, ('dp', 'expert')), may hold values from -6 to 6
- out_grad: bfloat16 [2, 8192, 768], P(None, ('dp', 'expert')), may hold values from -6 to 6
- segments: int32 [2, 8192], P(None, ('dp', 'expert')), may hold values from 0 to 2, as said below
- expert_ids: int32 [2, 8192, 1], P(None, ('dp', 'expert')), may hold values from 0 to 7; in each aligned block of 256 rows (0 to 255, 256 to 511, ..., all dimensions but the last counted through in order) at most 64 rows name the same one
- gate_values: float32 [2, 8192], P(None, ('dp', 'expert')), may hold values from 0.5 to 1
- norm_gains: float32 [2, 768], replicated, may hold values from 0.5 to 1.5
- rel_bias: float32 [32, 12], replicated, may hold values from -3 to 3
- qkv_weight: float32 [768, 2304], P(('dp', 'expert')), may hold values from -0.21875 to 0.21875
- proj_weight: float32 [768, 768], P(('dp', 'expert')), may hold values from -3.5 to 3.5
- expert_in: float32 [8, 768, 3072], P('expert', 'dp'), may hold values from -0.21875 to 0.21875
- expert_out: float32 [8, 3072, 768], P('expert', 'dp'), may hold values from -0.15625 to 0.15625
- first_gains: float32 [2, 768], replicated
- second_gains: float32 [2, 768], replicated, as said below
- first_bias: float32 [32, 12], replicated
- second_bias: float32 [32, 12], replicated, as said below
- first_qkv: float32 [768, 2304], P(('dp', 'expert'))
- second_qkv: float32 [768, 2304], P(('dp', 'expert')), as said below
- first_proj: float32 [768, 768], P(('dp', 'expert'))
- second_proj: float32 [768, 768], P(('dp', 'expert')), as said below
- first_in: float32 [8, 768, 3072], P('expert', 'dp')
- second_in: float32 [8, 768, 3072], P('expert', 'dp'), as said below
- first_out: float32 [8, 3072, 768], P('expert', 'dp')
- second_out: float32 [8, 3072, 768], P('expert', 'dp'), as said below
Outputs:
- block_out: float32 [2, 8192, 768], P(None, ('dp', 'expert'))
- input_grad: float32 [2, 8192, 768], P(None, ('dp', 'expert'))
- grad_gains: float32 [2, 768], replicated
- grad_bias: float32 [32, 12], replicated
- grad_qkv: float32 [768, 2304], P(('dp', 'expert'))
- grad_proj: float32 [768, 768], P(('dp', 'expert'))
- grad_in: float32 [8, 768, 3072], P('expert', 'dp')
- grad_out: float32 [8, 3072, 768], P('expert', 'dp')
- new_gains: float32 [2, 768], replicated
- updated_relative_bias: float32 [32, 12], replicated
- new_qkv: float32 [768, 2304], P(('dp', 'expert'))
- new_proj: float32 [768, 768], P(('dp', 'expert'))
- new_in: float32 [8, 768, 3072], P('expert', 'dp')
- new_out: float32 [8, 3072, 768], P('expert', 'dp')
- moment_gains: float32 [2, 768], replicated
- moment_bias: float32 [32, 12], replicated
- moment_qkv: float32 [768, 2304], P(('dp', 'expert'))
- moment_proj: float32 [768, 768], P(('dp', 'expert'))
- moment_in: float32 [8, 768, 3072], P('expert', 'dp')
- moment_out: float32 [8, 3072, 768], P('expert', 'dp')
The draws below stay inside these ranges and needn't reach their ends.
Inputs may be any that keep to these rules, and one draw needn't show every extreme that they name: `segments`: along each sequence of 1024 tokens the numbers never fall; number 1 begins within the sequence's first 256 tokens and ends within its last 256, so that numbers 0 and 2 are both present. `expert_ids`: in each aligned block of 256 tokens of a micro-batch (one device's tokens) at most 64 tokens name one expert. `second_gains`: Positive. `second_bias`: Positive. `second_qkv`: Positive. `second_proj`: Positive. `second_in`: Positive. `second_out`: Positive.
All inputs are finite; a program needn't handle non-finite values.
Results may differ from the reference program's by a relative error of at most 0.015.
Values may be sent and summed in bfloat16 or wider, within the bound.
A program may use at most 320 MiB of HBM per device.

```python
import math
from functools import partial
import jax
import jax.numpy as jnp
import numpy as np
from jax import lax

D = 768
HEADS = 12
HEAD_DIM = 64
FF = 3072
BUCKETS = 32
MICRO = 2
STEP = 10
TOK_DEV = 256
EXPERTS = 8
SEQ = 1024
TOKENS = 8192
CAP = 64
PROJ_FAN = 3


def token_count():
    return float(MICRO * TOKENS)


def signed_moment(key, extent, grad_sq):
    sign_key, size_key = jax.random.split(key)
    flip_sign = jax.random.randint(sign_key, extent, 0, 2).astype(jnp.float32) * 2.0 - 1.0
    spread = jax.random.uniform(size_key, extent, jnp.float32, 0.5, 1.5)
    return flip_sign * spread * jnp.sqrt(grad_sq) / 9.0


def square_moment(key, extent, grad_sq):
    spread = jnp.exp(jax.random.uniform(key, extent, jnp.float32, 0.0, math.log(4.0)))
    return spread * grad_sq / 999.0


def gains_square():
    return jnp.array([[3.0], [0.4]], jnp.float32) * token_count()


def draw_segments(key, part):
    key = jax.random.fold_in(key, 1)
    start_key, key_stop_position = jax.random.split(key)
    seq_count = MICRO * TOKENS // SEQ
    starts = jax.random.randint(start_key, (seq_count, 1), 1, TOK_DEV)
    endings = jax.random.randint(key_stop_position, (seq_count, 1), SEQ - TOK_DEV + 1, SEQ)
    position = jnp.arange(SEQ, dtype=jnp.int32)[None, :]
    numbers = (position >= starts).astype(jnp.int32) + (position >= endings).astype(jnp.int32)
    return numbers.reshape(MICRO, TOKENS)


def draw_first_gains(key, part):
    key = jax.random.fold_in(key, 11)
    return signed_moment(key, (2, D), gains_square())


def draw_second_gains(key, part):
    key = jax.random.fold_in(key, 12)
    return square_moment(key, (2, D), gains_square())


def draw_first_bias(key, part):
    key = jax.random.fold_in(key, 13)
    return signed_moment(key, (BUCKETS, HEADS), 0.25 * token_count())


def draw_second_bias(key, part):
    key = jax.random.fold_in(key, 14)
    return square_moment(key, (BUCKETS, HEADS), 0.25 * token_count())


def draw_first_qkv(key, part):
    key = jax.random.fold_in(key, 15)
    return signed_moment(key, (D, 3 * D), token_count())


def draw_second_qkv(key, part):
    key = jax.random.fold_in(key, 16)
    return square_moment(key, (D, 3 * D), token_count())


def draw_first_proj(key, part):
    key = jax.random.fold_in(key, 17)
    return signed_moment(key, (D, D), 3.0 * token_count() / SEQ)


def draw_second_proj(key, part):
    key = jax.random.fold_in(key, 18)
    return square_moment(key, (D, D), 3.0 * token_count() / SEQ)


def draw_first_in(key, part):
    key = jax.random.fold_in(key, 19)
    return signed_moment(key, (EXPERTS, D, FF), 0.1 * token_count() / EXPERTS)


def draw_second_in(key, part):
    key = jax.random.fold_in(key, 20)
    return square_moment(key, (EXPERTS, D, FF), 0.1 * token_count() / EXPERTS)


def draw_first_out(key, part):
    key = jax.random.fold_in(key, 21)
    return signed_moment(key, (EXPERTS, FF, D), 0.2 * token_count() / EXPERTS)


def draw_second_out(key, part):
    key = jax.random.fold_in(key, 22)
    return square_moment(key, (EXPERTS, FF, D), 0.2 * token_count() / EXPERTS)


def shard_levels(key, shape, shards, least, top_value):
    def one(axis_at, shards_of):
        heights = jax.random.uniform(jax.random.fold_in(jax.random.fold_in(key, 6), axis_at), (shards_of,), jnp.float32, least / len(shards), top_value / len(shards))
        return jnp.repeat(jnp.exp(heights), shape[axis_at] // shards_of).reshape((-1,) + (1,) * (len(shape) - axis_at - 1))

    factor_of = one(*shards[0])
    for cut in shards[1:]:
        factor_of = factor_of * one(*cut)
    return factor_of


def shared_out(stream_key, own, number, rows, number_of, top, limit, skew):
    ranking = jax.random.permutation(stream_key, number_of)
    crowded, usual = portions_of(number_of, rows * top, limit, skew, True), portions_of(number_of, rows * top, limit, skew, False)
    places = jnp.arange(number_of)

    def named(sizes, offset_by):
        used = int((sizes > 0).sum())
        fixed = max(1, used // 4)
        passed = fixed + (places - fixed + offset_by * (used - fixed)) % max(1, number_of - fixed)
        return jnp.zeros((number_of,), jnp.int32).at[ranking[jnp.where(places < fixed, places, passed)]].set(jnp.asarray(sizes, jnp.int32))

    sizes = jnp.where(number % 4 == 0, named(crowded, number // 4), named(usual, number - number // 4 - 1))
    mixed = jax.random.permutation(jax.random.fold_in(own, 3), number_of)
    giver, receiver = mixed[0:number_of // 2 * 2:2], mixed[1:number_of // 2 * 2:2]
    margin = jnp.minimum(sizes[giver] - 1, limit - sizes[receiver]) // 2
    margin = jnp.where((giver == ranking[0]) | (receiver == ranking[0]) | (sizes[receiver] == 0), 0, jnp.maximum(margin, 0))
    passed = jax.random.randint(jax.random.fold_in(own, 4), (number_of // 2,), 0, 1 << 20) % (margin + 1)
    sizes = sizes.at[giver].add(-passed).at[receiver].add(passed)
    members = jnp.searchsorted(jnp.cumsum(sizes), jnp.arange(rows * top), side="right").astype(jnp.int32)
    table = members.reshape(top, rows).T
    table = table[jax.random.permutation(jax.random.fold_in(own, 1), rows)]
    offset_by = jax.random.randint(jax.random.fold_in(own, 2), (rows, 1), 0, top)
    return jnp.take_along_axis(table, (jnp.arange(top)[None, :] + offset_by) % top, axis=1)


def portions_of(count, total, bound, skew, full):
    loads = [(1 << 20) // math.isqrt(grade ** skew) + 1 for grade in range(1, count + 1)]
    largest = bound if full else min(bound, max(-(-total // count), total * loads[0] // sum(loads)))
    least = 1 if total - largest >= count - 1 else 0
    given, spare = [largest] + [least] * (count - 1), total - largest - least * (count - 1)
    while spare > 0:
        movable = [i for i in range(1, count) if given[i] < largest] or [i for i in range(1, count) if given[i] < bound]
        whole, left = sum([loads[i] for i in movable]), spare
        for i in movable:
            extra = min(bound - given[i], max(1, left * loads[i] // whole), spare)
            given[i] = given[i] + extra
            spare = spare - extra
    return np.array(given)


def noise(rng, dims, width, bound, cuts=(), kind=jnp.bfloat16):
    drawn = jax.random.normal(rng, dims, jnp.float32) * width
    if len(cuts) > 0:
        drawn = shard_levels(rng, dims, cuts, -0.22, 0.18) * drawn
    return jnp.clip(drawn, min=-bound, max=bound).astype(kind)


def setup_inputs(seed: int = 0) -> dict:
    key_of = jax.random.split(jax.random.key(seed), 24)
    tokens_in = noise(key_of[0], (MICRO, TOKENS, D), 1.0, 6.0, ((1, 32),))
    out_grad = noise(key_of[1], (MICRO, TOKENS, D), 1.0, 6.0, ((1, 32),))
    segments = draw_segments(jax.random.fold_in(key_of[23], 71), 0)
    expert_ids_keys = jax.random.split(jax.random.fold_in(key_of[3], 1), MICRO * TOKENS // TOK_DEV)
    expert_ids_turns = jax.random.permutation(jax.random.fold_in(key_of[3], 3), MICRO * TOKENS // TOK_DEV)
    expert_ids = jax.vmap(lambda own, number: shared_out(jax.random.fold_in(key_of[3], 2), own, number, TOK_DEV, EXPERTS, 1, CAP, 2))(expert_ids_keys, expert_ids_turns).reshape((MICRO, TOKENS, 1))
    gate_values = jnp.clip(0.5 + 0.5 * jax.random.uniform(key_of[4], (MICRO, TOKENS), jnp.float32) ** shard_levels(key_of[4], (MICRO, TOKENS), ((1, 32),), -0.2, 0.2), 0.5, 1.0)
    norm_gains = jnp.clip(1.0 + 0.1 * jax.random.normal(key_of[5], (2, D), jnp.float32), 0.5, 1.5)
    rel_bias = noise(key_of[6], (BUCKETS, HEADS), 0.5, 3.0, (), jnp.float32)
    qkv_weight = noise(key_of[7], (D, 3 * D), D ** -0.5, 0.21875, ((0, 32),), jnp.float32)
    proj_weight = noise(key_of[8], (D, D), PROJ_FAN ** -0.5, 3.5, ((0, 32),), jnp.float32)
    expert_in = noise(key_of[9], (EXPERTS, D, FF), D ** -0.5, 0.21875, ((0, 4), (1, 8)), jnp.float32)
    expert_out = noise(key_of[10], (EXPERTS, FF, D), (FF // 2) ** -0.5, 0.15625, ((0, 4), (1, 8)), jnp.float32)
    first_gains = draw_first_gains(jax.random.fold_in(key_of[23], 71), 0)
    second_gains = draw_second_gains(jax.random.fold_in(key_of[23], 71), 0)
    first_bias = draw_first_bias(jax.random.fold_in(key_of[23], 71), 0)
    second_bias = draw_second_bias(jax.random.fold_in(key_of[23], 71), 0)
    first_qkv = draw_first_qkv(jax.random.fold_in(key_of[23], 71), 0)
    second_qkv = draw_second_qkv(jax.random.fold_in(key_of[23], 71), 0)
    first_proj = draw_first_proj(jax.random.fold_in(key_of[23], 71), 0)
    second_proj = draw_second_proj(jax.random.fold_in(key_of[23], 71), 0)
    first_in = draw_first_in(jax.random.fold_in(key_of[23], 71), 0)
    second_in = draw_second_in(jax.random.fold_in(key_of[23], 71), 0)
    first_out = draw_first_out(jax.random.fold_in(key_of[23], 71), 0)
    second_out = draw_second_out(jax.random.fold_in(key_of[23], 71), 0)
    return {"tokens_in": tokens_in, "out_grad": out_grad, "segments": segments, "expert_ids": expert_ids, "gate_values": gate_values, "norm_gains": norm_gains, "rel_bias": rel_bias, "qkv_weight": qkv_weight, "proj_weight": proj_weight, "expert_in": expert_in, "expert_out": expert_out, "first_gains": first_gains, "second_gains": second_gains, "first_bias": first_bias, "second_bias": second_bias, "first_qkv": first_qkv, "second_qkv": second_qkv, "first_proj": first_proj, "second_proj": second_proj, "first_in": first_in, "second_in": second_in, "first_out": first_out, "second_out": second_out}


EPS_NORM = 1e-06
MASKED = -1000000000.0
LIMITS = (12, 16, 23, 32, 46, 64, 91)
UPPER_PRECISION = lax.Precision.HIGHEST

@jax.custom_vjp
def low(v):
    return lax.optimization_barrier(v.astype(jnp.bfloat16)).astype(jnp.float32)

@jax.custom_vjp
def low_back(v):
    return v

def low_keep(v):
    return (low(v), None)

def low_pass(kept, grad):
    return (grad,)

def back_keep(v):
    return (v, None)

def back_low(kept, grad):
    return (low(grad),)
low.defvjp(low_keep, low_pass)
low_back.defvjp(back_keep, back_low)

def matmul(left, right):
    return jnp.dot(left, right, precision=UPPER_PRECISION)

def rms_norm(inputs, gain_vec):
    inv_rms = lax.rsqrt(lax.optimization_barrier(jnp.mean(inputs * inputs, axis=-1, keepdims=True)) + EPS_NORM)
    return inputs * inv_rms * gain_vec

def bucket_of(query_position_index, key_position_index):
    offset = key_position_index[None, :] - query_position_index[:, None]
    distance = jnp.abs(offset)
    far_bucket = 8 + sum(((distance >= bound_at).astype(jnp.int32) for bound_at in LIMITS))
    return (jnp.where(distance < 8, distance, far_bucket) + jnp.where(offset > 0, 16, 0)).astype(jnp.int32)

def slot_index(chosen, expert_count, capacity):
    hot_rows = (chosen[:, None] == jnp.arange(expert_count, dtype=jnp.int32)[None, :]).astype(jnp.int32)
    rank_in = lax.optimization_barrier(jnp.sum((jnp.cumsum(hot_rows, axis=0) - 1) * hot_rows, axis=1))
    return (chosen * capacity + rank_in).astype(jnp.int32)

def adam_step(weight, gradient, first_mom, second, step_rate):
    first_new = 0.9 * first_mom + 0.1 * gradient
    second_new = 0.999 * second + 0.001 * gradient * gradient
    first_hat = first_new / (1.0 - 0.9 ** STEP)
    second_hat = second_new / (1.0 - 0.999 ** STEP)
    updated = weight - step_rate * (first_hat / (jnp.sqrt(second_hat) + 1e-08) + 0.01 * weight)
    return (updated, second_new)

def attend(bias_lookup_table, bucket_map, operands):
    queries, keys_seq, values_seq, seg_seq = operands
    raw_scores = jnp.einsum('qhd,khd->hqk', queries, keys_seq, precision=UPPER_PRECISION)
    bias_now = jnp.transpose(bias_lookup_table[bucket_map], (2, 0, 1))
    allowed = seg_seq[:, None] == seg_seq[None, :]
    logits = jnp.where(allowed[None], HEAD_DIM ** (-0.5) * low_back(raw_scores) + bias_now, MASKED)
    row_max = lax.optimization_barrier(jnp.max(logits, axis=-1, keepdims=True))
    log_total = row_max + jnp.log(lax.optimization_barrier(jnp.sum(jnp.exp(logits - row_max), axis=-1, keepdims=True)))
    attn_probs = jnp.exp(logits - log_total)
    return jnp.einsum('hqk,khd->qhd', low(attn_probs), values_seq, precision=UPPER_PRECISION)

def expert_apply(operands):
    rows_in, in_mat, out_mat = operands
    pre_act = low_back(matmul(rows_in, low(in_mat)))
    post_act = low(jax.nn.gelu(pre_act, approximate=False))
    return low_back(low(matmul(post_act, low(out_mat))))

def micro_forward(residual, seg_row, slot_rows, gate_row, gains, bias_lookup_table, qkv_w, proj_w, in_w, out_w):
    seq_count = TOKENS // SEQ
    blocks = TOKENS // TOK_DEV
    positions = jnp.arange(SEQ, dtype=jnp.int32)
    bucket_map = bucket_of(positions, positions)
    normed = low(rms_norm(residual, gains[0]))
    qkv_all = low_back(low(matmul(normed, low(qkv_w))))
    queries = qkv_all[:, :D].reshape(seq_count, SEQ, HEADS, HEAD_DIM)
    keys_all = qkv_all[:, D:2 * D].reshape(seq_count, SEQ, HEADS, HEAD_DIM)
    values_all = qkv_all[:, 2 * D:].reshape(seq_count, SEQ, HEADS, HEAD_DIM)
    attended = lax.map(jax.checkpoint(partial(attend, bias_lookup_table, bucket_map)), (queries, keys_all, values_all, seg_row.reshape(seq_count, SEQ)))
    mixed_out = low_back(low(attended.reshape(TOKENS, D)))
    hidden = residual + low_back(matmul(mixed_out, low(proj_w)))
    routed = low_back(low(rms_norm(hidden, gains[1])))
    block_rows = jnp.arange(blocks, dtype=jnp.int32)[:, None]
    buffer = jnp.zeros((blocks, EXPERTS * CAP, D), jnp.float32).at[block_rows, slot_rows].set(routed.reshape(blocks, TOK_DEV, D))
    per_expert = jnp.transpose(buffer.reshape(blocks, EXPERTS, CAP, D), (1, 0, 2, 3)).reshape(EXPERTS, blocks * CAP, D)
    results = lax.map(jax.checkpoint(expert_apply), (per_expert, in_w, out_w))
    back_buf = jnp.transpose(results.reshape(EXPERTS, blocks, CAP, D), (1, 0, 2, 3)).reshape(blocks, EXPERTS * CAP, D)
    picked = back_buf[block_rows, slot_rows].reshape(TOKENS, D)
    return hidden + gate_row[:, None] * picked

def reference(tokens_in, out_grad, segments, expert_ids, gate_values, norm_gains, rel_bias, qkv_weight, proj_weight, expert_in, expert_out, first_gains, second_gains, first_bias, second_bias, first_qkv, second_qkv, first_proj, second_proj, first_in, second_in, first_out, second_out):
    blocks = TOKENS // TOK_DEV

    def slot_block(chosen):
        return slot_index(chosen, EXPERTS, CAP)
    slots_all = jax.vmap(slot_block)(expert_ids.reshape(MICRO * blocks, TOK_DEV).astype(jnp.int32)).reshape(MICRO, blocks, TOK_DEV)

    def forward(resid_all, gains, bias_lookup_table, qkv_w, proj_w, in_w, out_w):
        outputs = []
        for micro_idx in range(MICRO):
            outputs.append(micro_forward(resid_all[micro_idx], segments[micro_idx], slots_all[micro_idx], gate_values[micro_idx], gains, bias_lookup_table, qkv_w, proj_w, in_w, out_w))
        return jnp.stack(outputs)
    resid_all = tokens_in.astype(jnp.float32)
    block_out, pullback = jax.vjp(forward, resid_all, norm_gains, rel_bias, qkv_weight, proj_weight, expert_in, expert_out)
    input_grad, grad_gains, grad_bias, grad_qkv, grad_proj, grad_in, grad_out = pullback(out_grad.astype(jnp.float32))
    new_gains, moment_gains = adam_step(norm_gains, grad_gains, first_gains, second_gains, 0.25)
    updated_relative_bias, moment_bias = adam_step(rel_bias, grad_bias, first_bias, second_bias, 0.5)
    new_qkv, moment_qkv = adam_step(qkv_weight, grad_qkv, first_qkv, second_qkv, D ** (-0.5))
    new_proj, moment_proj = adam_step(proj_weight, grad_proj, first_proj, second_proj, PROJ_FAN ** (-0.5))
    new_in, moment_in = adam_step(expert_in, grad_in, first_in, second_in, D ** (-0.5))
    new_out, moment_out = adam_step(expert_out, grad_out, first_out, second_out, (FF // 2) ** (-0.5))
    return (block_out, input_grad, grad_gains, grad_bias, grad_qkv, grad_proj, grad_in, grad_out, new_gains, updated_relative_bias, new_qkv, new_proj, new_in, new_out, moment_gains, moment_bias, moment_qkv, moment_proj, moment_in, moment_out)
```

```python
import functools

import jax
import jax.numpy as jnp
from jax import lax
from jax.experimental import pallas as pl
from jax.experimental.pallas import tpu as pltpu
from jax.sharding import PartitionSpec as P

BUCKETS = 32
STEP = 10


EPS_NORM = 1e-06
MASKED = -1000000000.0
LIMITS = (12, 16, 23, 32, 46, 64, 91)
UPPER_PRECISION = lax.Precision.HIGHEST
LANES = 128
STRIP = 8
VMEM_BYTES = 48 * 1024 * 1024


def rms_norm(inputs, gain_vec):
    inv_rms = lax.rsqrt(jnp.mean(inputs * inputs, axis=-1, keepdims=True) + EPS_NORM)
    return inputs * inv_rms * gain_vec


def strip_onehot(first_query, tok_rows, seq_len):
    width = seq_len + tok_rows
    column = jnp.arange(width, dtype=jnp.int32)[None, :]
    row = jnp.arange(STRIP, dtype=jnp.int32)[:, None]
    offset = jnp.where(column >= seq_len, column - width, column) - row - first_query
    distance = jnp.abs(offset)
    far_bucket = 8 + sum(((distance >= bound_at).astype(jnp.int32) for bound_at in LIMITS))
    buckets = jnp.where(distance < 8, distance, far_bucket) + jnp.where(offset > 0, 16, 0)
    return (buckets[None] == jnp.arange(BUCKETS, dtype=jnp.int32)[:, None, None]).astype(
        jnp.float32
    )


def spread_bias(strip, rows, seq_len):
    grown = strip
    have = STRIP
    while have < rows:
        grown = jnp.concatenate([grown, pltpu.roll(grown, have, axis=1)], axis=0)
        have *= 2
    return grown[:, :seq_len]


def gather_bias(block, rows, width):
    left = jnp.concatenate(
        [block, jnp.zeros((rows, width - block.shape[1]), jnp.float32)], axis=1
    )
    have = rows
    while have > STRIP:
        have //= 2
        left = left[:have] + pltpu.roll(left[have:], width - have, axis=1)
    return left


def head_mask(which, head_dim):
    lane = lax.broadcasted_iota(jnp.int32, (1, LANES), 1)
    return ((lane >= which * head_dim) & (lane < (which + 1) * head_dim)).astype(jnp.float32)


def only_head(block, mask):
    return (block.astype(jnp.float32) * mask).astype(jnp.bfloat16)


def product(left, right, left_dim, right_dim):
    return lax.dot_general(
        left, right, (((left_dim,), (right_dim,)), ((), ())), preferred_element_type=jnp.float32
    )


def attend_kernel(head_dim, q_ref, k_ref, v_ref, sq_ref, sk_ref, strip_ref, o_ref, lse_ref):
    rows, seq_len = (q_ref.shape[1], k_ref.shape[1])
    allowed = sq_ref[0] == sk_ref[0]
    out = jnp.zeros((rows, LANES), jnp.float32)
    lse = jnp.zeros((rows, LANES), jnp.float32)
    for which in range(LANES // head_dim):
        mask = head_mask(which, head_dim)
        raw = product(only_head(q_ref[0], mask), k_ref[0], 1, 1)
        bias = spread_bias(strip_ref[which], rows, seq_len)
        logits = jnp.where(allowed, head_dim ** (-0.5) * raw + bias, MASKED)
        top = jnp.max(logits, axis=1, keepdims=True)
        weights = jnp.exp(logits - top)
        total = jnp.sum(weights, axis=1, keepdims=True)
        mixed = product(weights.astype(jnp.bfloat16), v_ref[0], 1, 0)
        out = out + mixed * (1.0 / total) * mask
        lse = lse + (top + jnp.log(total)) * mask
    o_ref[0] = out.astype(jnp.bfloat16)
    lse_ref[0] = lse


def attend_back_kernel(
    head_dim,
    q_ref,
    k_ref,
    v_ref,
    do_ref,
    lse_ref,
    sq_ref,
    sk_ref,
    strip_ref,
    dq_ref,
    dkv_ref,
    diag_ref,
):
    rows, seq_len = (q_ref.shape[1], k_ref.shape[1])
    width = strip_ref.shape[2]
    allowed = sq_ref[0] == sk_ref[0]
    grad_q = jnp.zeros((rows, LANES), jnp.float32)
    grad_k = jnp.zeros((seq_len, LANES), jnp.float32)
    grad_v = jnp.zeros((seq_len, LANES), jnp.float32)
    for which in range(LANES // head_dim):
        mask = head_mask(which, head_dim)
        raw = product(only_head(q_ref[0], mask), k_ref[0], 1, 1)
        bias = spread_bias(strip_ref[which], rows, seq_len)
        logits = jnp.where(allowed, head_dim ** (-0.5) * raw + bias, MASKED)
        lse = lse_ref[0, :, which * head_dim : which * head_dim + 1]
        probs = jnp.exp(logits - lse)
        grad_probs = product(only_head(do_ref[0], mask), v_ref[0], 1, 1)
        center = jnp.sum(probs * grad_probs, axis=1, keepdims=True)
        grad_logits = probs * (grad_probs - center)
        diag_ref[0, which] = gather_bias(grad_logits, rows, width)
        grad_raw = (head_dim ** (-0.5) * grad_logits).astype(jnp.bfloat16)
        grad_q = grad_q + product(grad_raw, k_ref[0], 1, 0) * mask
        grad_k = grad_k + product(grad_raw, q_ref[0], 0, 0) * mask
        grad_v = grad_v + product(probs.astype(jnp.bfloat16), do_ref[0], 0, 0) * mask
    dq_ref[0] = grad_q.astype(jnp.bfloat16)
    dkv_ref[0, 0] = grad_k.astype(jnp.bfloat16)
    dkv_ref[1, 0] = grad_v.astype(jnp.bfloat16)


def attention_specs(rows, seq_len, pairs, per_block, width):
    return dict(
        q=pl.BlockSpec((1, rows, LANES), lambda m, p: (m, 0, p)),
        k=pl.BlockSpec((1, seq_len, LANES), lambda m, p: (m, 0, p)),
        v=pl.BlockSpec((1, seq_len, LANES), lambda m, p: (m, 0, pairs + p)),
        sq=pl.BlockSpec((1, rows, 1), lambda m, p: (m, 0, 0)),
        sk=pl.BlockSpec((1, 1, seq_len), lambda m, p: (m, 0, 0)),
        strip=pl.BlockSpec((per_block, STRIP, width), lambda m, p: (p, 0, 0)),
    )


def attention(qkv_all, kv_all, seg_q, seg_k, strips, head_dim):
    micros, rows, _ = qkv_all.shape
    seq_len = kv_all.shape[1]
    heads, _, width = strips.shape
    model_width = heads * head_dim
    per_block = LANES // head_dim
    pairs = heads // per_block
    sp = attention_specs(rows, seq_len, pairs, per_block, width)
    return pl.pallas_call(
        functools.partial(attend_kernel, head_dim),
        grid=(micros, pairs),
        in_specs=[sp["q"], sp["k"], sp["v"], sp["sq"], sp["sk"], sp["strip"]],
        out_specs=[sp["q"], sp["q"]],
        out_shape=[
            jax.ShapeDtypeStruct((micros, rows, model_width), jnp.bfloat16),
            jax.ShapeDtypeStruct((micros, rows, model_width), jnp.float32),
        ],
        compiler_params=pltpu.CompilerParams(vmem_limit_bytes=VMEM_BYTES),
        cost_estimate=pl.CostEstimate(
            flops=16 * micros * heads * rows * seq_len * LANES,
            bytes_accessed=4 * micros * seq_len * model_width * 2,
            transcendentals=micros * heads * rows * seq_len,
        ),
    )(qkv_all, kv_all, kv_all, seg_q, seg_k, strips)


def attention_back(qkv_all, kv_all, grad_mixed, lse, seg_q, seg_k, strips, head_dim):
    micros, rows, _ = qkv_all.shape
    seq_len = kv_all.shape[1]
    heads, _, width = strips.shape
    model_width = heads * head_dim
    per_block = LANES // head_dim
    pairs = heads // per_block
    sp = attention_specs(rows, seq_len, pairs, per_block, width)
    return pl.pallas_call(
        functools.partial(attend_back_kernel, head_dim),
        grid=(micros, pairs),
        in_specs=[
            sp["q"], sp["k"], sp["v"], sp["q"], sp["q"], sp["sq"], sp["sk"], sp["strip"],
        ],
        out_specs=[
            sp["q"],
            pl.BlockSpec((2, 1, seq_len, LANES), lambda m, p: (0, m, 0, p)),
            pl.BlockSpec((1, per_block, STRIP, width), lambda m, p: (m, p, 0, 0)),
        ],
        out_shape=[
            jax.ShapeDtypeStruct((micros, rows, model_width), jnp.bfloat16),
            jax.ShapeDtypeStruct((2, micros, seq_len, model_width), jnp.bfloat16),
            jax.ShapeDtypeStruct((micros, heads, STRIP, width), jnp.float32),
        ],
        compiler_params=pltpu.CompilerParams(vmem_limit_bytes=VMEM_BYTES),
        cost_estimate=pl.CostEstimate(
            flops=40 * micros * heads * rows * seq_len * LANES,
            bytes_accessed=8 * micros * seq_len * model_width * 2,
            transcendentals=micros * heads * rows * seq_len,
        ),
    )(qkv_all, kv_all, kv_all, grad_mixed, lse, seg_q, seg_k, strips)


def slot_rank(chosen, expert_count):
    hot_rows = (chosen[:, :, None] == jnp.arange(expert_count, dtype=jnp.int32)).astype(jnp.int32)
    return jnp.sum((jnp.cumsum(hot_rows, axis=1) - 1) * hot_rows, axis=2)


def adam_step(weight, gradient, first_mom, second, step_rate):
    first_new = 0.9 * first_mom + 0.1 * gradient
    second_new = 0.999 * second + 0.001 * gradient * gradient
    first_hat = first_new / (1.0 - 0.9**STEP)
    second_hat = second_new / (1.0 - 0.999**STEP)
    updated = weight - step_rate * (first_hat / (jnp.sqrt(second_hat) + 1e-08) + 0.01 * weight)
    return (updated, second_new)


def local(
    tokens_in,
    out_grad,
    segments,
    expert_ids,
    gate_values,
    norm_gains,
    rel_bias,
    qkv_weight,
    proj_weight,
    expert_in,
    expert_out,
    first_gains,
    second_gains,
    first_bias,
    second_bias,
    first_qkv,
    second_qkv,
    first_proj,
    second_proj,
    first_in,
    second_in,
    first_out,
    second_out,
):
    groups = lax.axis_size("expert")
    slices = lax.axis_size("dp")
    micros, tok_rows, model_width = tokens_in.shape
    seq_len = tok_rows * groups
    head_count = rel_bias.shape[1]
    head_dim = model_width // head_count
    local_experts = expert_in.shape[0]
    expert_count = local_experts * groups
    capacity = 2 * tok_rows // expert_count
    hidden_units = expert_in.shape[2]
    own_rows = qkv_weight.shape[0]
    dense_width = 4 * model_width
    f32, bf16 = (jnp.float32, jnp.bfloat16)

    dense_low = jnp.concatenate([qkv_weight.astype(bf16), proj_weight.astype(bf16)], axis=1)
    dense_part = lax.all_gather(dense_low, "dp", axis=0, tiled=False)
    in_low, dense_part = lax.optimization_barrier((expert_in.astype(bf16), dense_part))
    dense_all = lax.all_gather(dense_part, "expert", axis=1, tiled=False).reshape(
        model_width, dense_width
    )
    dense_qkv = dense_all[:, : 3 * model_width]
    dense_proj = dense_all[:, 3 * model_width :]
    exp_in = lax.all_gather(in_low, "dp", axis=1, tiled=True)
    out_low, exp_in = lax.optimization_barrier((expert_out.astype(bf16), exp_in))
    exp_out = lax.all_gather(out_low, "dp", axis=1, tiled=True)

    onehot = strip_onehot(lax.axis_index("expert") * tok_rows, tok_rows, seq_len)
    strips = jnp.einsum("vg,vrc->grc", rel_bias, onehot, precision=UPPER_PRECISION)
    residual = tokens_in.astype(f32)
    normed, norm_back_one = jax.vjp(rms_norm, residual, norm_gains[0])
    act_one = normed.astype(bf16)
    qkv_all = jnp.einsum("mtd,df->mtf", act_one, dense_qkv, preferred_element_type=f32).astype(
        bf16
    )
    seg_cols = jnp.broadcast_to(segments.astype(bf16)[:, :, None], (micros, tok_rows, LANES))
    kv_all = lax.all_gather(
        jnp.concatenate([qkv_all[:, :, model_width:], seg_cols], axis=2),
        "expert",
        axis=1,
        tiled=True,
    )
    seg_q = segments.astype(f32)[:, :, None]
    seg_k = kv_all[:, :, 2 * model_width].astype(f32)[:, None, :]
    mixed_out, lse = attention(qkv_all, kv_all, seg_q, seg_k, strips, head_dim)
    hidden = residual + jnp.einsum(
        "mtd,df->mtf", mixed_out, dense_proj, preferred_element_type=f32
    )
    normed_two, norm_back_two = jax.vjp(rms_norm, hidden, norm_gains[1])

    chosen = expert_ids[:, :, 0]
    slot_rows = chosen * capacity + slot_rank(chosen, expert_count)
    place = (
        jnp.arange(expert_count * capacity, dtype=jnp.int32)[None, :, None]
        == slot_rows[:, None, :]
    ).astype(bf16)

    def to_experts(rows_low):
        buf = jnp.einsum("mst,mtd->msd", place, rows_low, preferred_element_type=f32).astype(bf16)
        buf = buf.reshape(micros, groups, local_experts, capacity, model_width)
        got = lax.all_to_all(buf, "expert", split_axis=1, concat_axis=1, tiled=True)
        return jnp.transpose(got, (2, 0, 1, 3, 4)).reshape(
            local_experts, micros * groups * capacity, model_width
        )

    def from_experts(rows_low):
        buf = jnp.transpose(
            rows_low.reshape(local_experts, micros, groups, capacity, model_width), (1, 2, 0, 3, 4)
        )
        got = lax.all_to_all(buf, "expert", split_axis=1, concat_axis=1, tiled=True)
        got = got.reshape(micros, expert_count * capacity, model_width)
        return jnp.einsum("mst,msd->mtd", place, got, preferred_element_type=f32)

    gate_col = gate_values[:, :, None]
    grad_top = out_grad.astype(f32)
    grad_res = to_experts((gate_col * grad_top).astype(bf16))
    arrived = to_experts(normed_two.astype(bf16))
    pre_act = jnp.einsum("ecd,edf->ecf", arrived, exp_in, preferred_element_type=f32)
    cdf = 0.5 * lax.erfc(-pre_act * (0.5**0.5))
    slope = cdf + pre_act * (jnp.exp(-0.5 * pre_act * pre_act) * 0.3989422804014327)
    post_act, slope = lax.optimization_barrier(
        ((pre_act * cdf).astype(bf16), slope.astype(bf16))
    )
    part_out = jnp.einsum(
        "ecf,ecd->efd", post_act, grad_res, preferred_element_type=f32
    ).astype(bf16)
    part_out, exp_out = lax.optimization_barrier((part_out, exp_out))
    grad_out = lax.psum_scatter(part_out, "dp", scatter_dimension=1, tiled=True).astype(f32)
    grad_post = jnp.einsum("ecd,efd->ecf", grad_res, exp_out, preferred_element_type=f32)
    grad_pre = (grad_post * slope.astype(f32)).astype(bf16)
    part_in = jnp.einsum("ecd,ecf->edf", arrived, grad_pre, preferred_element_type=f32).astype(
        bf16
    )
    grad_in = lax.psum_scatter(part_in, "dp", scatter_dimension=1, tiled=True).astype(f32)
    grad_back = from_experts(
        jnp.einsum("ecf,edf->ecd", grad_pre, exp_in, preferred_element_type=f32).astype(bf16)
    )
    result = from_experts(
        jnp.einsum("ecf,efd->ecd", post_act, exp_out, preferred_element_type=f32).astype(bf16)
    )
    block_out = hidden + gate_col * result

    grad_hidden_n, grad_gain_two = norm_back_two(grad_back)
    grad_hidden = grad_top + grad_hidden_n
    grad_attn = grad_hidden.astype(bf16)
    part_proj = jnp.einsum("mtd,mtf->df", mixed_out, grad_attn, preferred_element_type=f32)
    grad_mixed = jnp.einsum(
        "mtf,df->mtd", grad_attn, dense_proj, preferred_element_type=f32
    ).astype(bf16)
    grad_query, grad_kv, diag = attention_back(
        qkv_all, kv_all, grad_mixed, lse, seg_q, seg_k, strips, head_dim
    )
    part_table = jnp.einsum(
        "grc,vrc->vg", jnp.sum(diag, axis=0), onehot, precision=UPPER_PRECISION
    )
    kv_terms = lax.all_to_all(
        grad_kv.reshape(2, micros, groups, tok_rows, model_width),
        "expert",
        split_axis=2,
        concat_axis=2,
        tiled=True,
    )
    kv_sum = jnp.sum(kv_terms.astype(f32), axis=2).astype(bf16)
    grad_qkv_rows = jnp.concatenate([grad_query, kv_sum[0], kv_sum[1]], axis=2)
    part_qkv = jnp.einsum("mtd,mtf->df", act_one, grad_qkv_rows, preferred_element_type=f32)
    grad_normed = jnp.einsum(
        "mtf,df->mtd", grad_qkv_rows, dense_qkv, preferred_element_type=f32
    )
    grad_resid_n, grad_gain_one = norm_back_one(grad_normed)
    input_grad = grad_hidden + grad_resid_n

    part_dense = jnp.concatenate([part_qkv, part_proj], axis=1).astype(bf16)
    part_dense = lax.all_to_all(
        part_dense.reshape(slices, groups, own_rows, dense_width),
        "expert",
        split_axis=1,
        concat_axis=1,
        tiled=True,
    )
    part_dense = jnp.sum(part_dense.astype(f32), axis=1).astype(bf16)
    part_dense = lax.all_to_all(part_dense, "dp", split_axis=0, concat_axis=0, tiled=True)
    grad_dense = jnp.sum(part_dense.astype(f32), axis=0)
    grad_qkv = grad_dense[:, : 3 * model_width]
    grad_proj = grad_dense[:, 3 * model_width :]
    grad_gains, grad_bias = lax.psum(
        (jnp.stack([grad_gain_one, grad_gain_two]), part_table), ("dp", "expert")
    )
    fan_proj = max(1, 4 * model_width // seq_len)
    new_gains, moment_gains = adam_step(norm_gains, grad_gains, first_gains, second_gains, 0.25)
    updated_relative_bias, moment_bias = adam_step(
        rel_bias, grad_bias, first_bias, second_bias, 0.5
    )
    new_qkv, moment_qkv = adam_step(
        qkv_weight, grad_qkv, first_qkv, second_qkv, model_width ** (-0.5)
    )
    new_proj, moment_proj = adam_step(
        proj_weight, grad_proj, first_proj, second_proj, fan_proj ** (-0.5)
    )
    new_in, moment_in = adam_step(expert_in, grad_in, first_in, second_in, model_width ** (-0.5))
    new_out, moment_out = adam_step(
        expert_out, grad_out, first_out, second_out, (hidden_units // 2) ** (-0.5)
    )
    return (
        block_out,
        input_grad,
        grad_gains,
        grad_bias,
        grad_qkv,
        grad_proj,
        grad_in,
        grad_out,
        new_gains,
        updated_relative_bias,
        new_qkv,
        new_proj,
        new_in,
        new_out,
        moment_gains,
        moment_bias,
        moment_qkv,
        moment_proj,
        moment_in,
        moment_out,
    )


def solution(mesh):
    placed = (
        P(None, ("dp", "expert"), None),
        P(None, ("dp", "expert"), None),
        P(None, ("dp", "expert")),
        P(None, ("dp", "expert"), None),
        P(None, ("dp", "expert")),
        P(),
        P(),
        P(("dp", "expert"), None),
        P(("dp", "expert"), None),
        P("expert", "dp", None),
        P("expert", "dp", None),
        P(),
        P(),
        P(),
        P(),
        P(("dp", "expert"), None),
        P(("dp", "expert"), None),
        P(("dp", "expert"), None),
        P(("dp", "expert"), None),
        P("expert", "dp", None),
        P("expert", "dp", None),
        P("expert", "dp", None),
        P("expert", "dp", None),
    )
    return jax.shard_map(
        local,
        mesh=mesh,
        in_specs=placed,
        out_specs=(
            P(None, ("dp", "expert"), None),
            P(None, ("dp", "expert"), None),
            P(),
            P(),
            P(("dp", "expert"), None),
            P(("dp", "expert"), None),
            P("expert", "dp", None),
            P("expert", "dp", None),
            P(),
            P(),
            P(("dp", "expert"), None),
            P(("dp", "expert"), None),
            P("expert", "dp", None),
            P("expert", "dp", None),
            P(),
            P(),
            P(("dp", "expert"), None),
            P(("dp", "expert"), None),
            P("expert", "dp", None),
            P("expert", "dp", None),
        ),
        check_vma=False,
    )
```
